256 devices in a mesh: row: 16 (over x, z_lo, core), col: 16 (over y, z_hi).
Axes of the slice: x: 4, y: 4, z: 8 (z_hi: 4, z_lo: 2; z = z_hi * 2 + z_lo), core: 2. Of those that a mesh axis runs over, the one named last changes fastest.
Arguments:
- vectors: float32 [262144, 128], P(('col', 'row')), may hold values from -6 to 6
- tile_values: bfloat16 [16, 16, 22, 512, 512], P('row', 'col'), may hold values from 0 to 1
- tile_rows: int32 [16, 16, 22], P('row', 'col'), may hold values from 0 to 31, as said below
- tile_cols: int32 [16, 16, 22], P('row', 'col'), may hold values from 0 to 31
- tile_count: int32 [16, 16], P('row', 'col'), may hold values from 1 to 22, as said below
- degrees: int32 [262144], replicated, may hold values from 16 to 255
Outputs:
- result: float32 [262144, 128], P(('row', 'col'))
The draws below stay inside these ranges and needn't reach their ends.
Inputs may be any that keep to these rules, and one draw needn't show every extreme that they name: `tile_rows`: within one device no two slots name the same pair of tile row and tile column. `tile_count`: some device has all 22 slots live.
All inputs are finite; a program needn't handle non-finite values.
Results may differ from the reference program's by a relative error of at most 0.0003.
Values sent between devices are 32-bit elements; how exact they have to be, the bound alone decides.
No kernel may reach another device: no remote copies, remote signals or barrier semaphores. Data moves between devices by JAX's collectives and lax.ppermute only.
A program may use at most 128 MiB of HBM per device.

```python
import jax
import jax.numpy as jnp
from jax import lax

TS = 512
V = 128
TILES_DEV = 22
ROW_TILES = 32
COL_TILES = 32
NODES = 262144
N_ROW = 16
N_COL = 16


def tile_places(key):
    sub_key = jax.random.fold_in(key, 7)
    dev_keys = jax.random.split(sub_key, N_ROW * N_COL)

    def pick_places(dev_key):
        return jax.random.permutation(dev_key, ROW_TILES * COL_TILES)[:TILES_DEV]
    places = jax.vmap(pick_places)(dev_keys)
    return places.reshape(N_ROW, N_COL, TILES_DEV).astype(jnp.int32)


def draw_tile_rows(key, part):
    return (tile_places(key) // COL_TILES).astype(jnp.int32)


def draw_tile_cols(key, part):
    return (tile_places(key) % COL_TILES).astype(jnp.int32)


def draw_tile_count(key, part):
    first_key, second_key = jax.random.split(jax.random.fold_in(key, 11))
    draw_base = jax.random.randint(first_key, (N_ROW * N_COL,), 0, TILES_DEV)
    counts = 1 + draw_base * draw_base // TILES_DEV
    full_device = jax.random.randint(second_key, (), 0, N_ROW * N_COL)
    flat_counts = jnp.where(jnp.arange(N_ROW * N_COL) == full_device, TILES_DEV, counts)
    return flat_counts.reshape(N_ROW, N_COL).astype(jnp.int32)


def draw_degrees(key, part):
    first_key, second_key = jax.random.split(jax.random.fold_in(key, 13))
    exponent = jax.random.randint(first_key, (NODES,), 0, 4)
    low_end = jnp.left_shift(jnp.full((NODES,), 16, jnp.int32), exponent.astype(jnp.int32))
    offset_add = jax.random.randint(second_key, (NODES,), 0, low_end)
    return (low_end + offset_add).astype(jnp.int32)


def level_of(stream_key, extent, cuts, least, largest):
    loudness, own = 1.0, jax.random.fold_in(stream_key, 6)
    for position, shards_of in cuts:
        draws = jnp.exp(jax.random.uniform(jax.random.fold_in(own, position), (shards_of,), jnp.float32, least / len(cuts), largest / len(cuts)))
        loudness = loudness * jnp.repeat(draws, extent[position] // shards_of).reshape([-1 if axis == position else 1 for axis in range(len(extent))])
    return loudness


def noise(rng, shape, spread, bound, cuts=(), kind=jnp.bfloat16):
    entries = spread * jax.random.normal(rng, shape, jnp.float32)
    if cuts:
        entries = entries * level_of(rng, shape, cuts, -0.22, 0.18)
    return jnp.clip(entries, -bound, bound).astype(kind)


def setup_inputs(seed: int = 0) -> dict:
    splits = jax.random.split(jax.random.key(seed), 7)
    vectors = noise(splits[0], (NODES, V), 1.0, 6.0, ((0, 256),), jnp.float32)
    tile_values = jnp.clip(1.0 * jax.random.uniform(splits[1], (N_ROW, N_COL, TILES_DEV, TS, TS), jnp.float32) ** level_of(splits[1], (N_ROW, N_COL, TILES_DEV, TS, TS), ((0, 16), (1, 16)), -0.2, 0.2), 0.0, 1.0).astype(jnp.bfloat16)
    tile_rows = draw_tile_rows(jax.random.fold_in(splits[6], 71), 0)
    tile_cols = draw_tile_cols(jax.random.fold_in(splits[6], 71), 0)
    tile_count = draw_tile_count(jax.random.fold_in(splits[6], 71), 0)
    degrees = draw_degrees(jax.random.fold_in(splits[6], 71), 0)
    return {"vectors": vectors, "tile_values": tile_values, "tile_rows": tile_rows, "tile_cols": tile_cols, "tile_count": tile_count, "degrees": degrees}


def reference(vectors, tile_values, tile_rows, tile_cols, tile_count, degrees):
    inv_root = lax.rsqrt(degrees.astype(jnp.float32))
    scaled = (vectors * inv_root[:, None]).reshape(NODES // TS, TS, V)
    devices = N_ROW * N_COL
    device_ids = jnp.arange(devices, dtype=jnp.int32)
    slot_ids = jnp.arange(TILES_DEV, dtype=jnp.int32)

    def add_device(summed, device_item):
        tile_block, row_ids, col_ids, live_count, device_id = device_item
        row_block = device_id // N_COL
        col_block = device_id % N_COL
        chosen = scaled[(col_block * COL_TILES + col_ids).astype(jnp.int32)]
        contrib = jnp.einsum('kij,kjv->kiv', tile_block.astype(jnp.float32), chosen.astype(jnp.float32), precision=lax.Precision.HIGHEST)
        live_mask = (slot_ids < live_count).astype(jnp.float32)
        contrib = contrib * live_mask[:, None, None]
        summed = summed.at[(row_block * ROW_TILES + row_ids).astype(jnp.int32)].add(contrib)
        return (summed, None)
    start = jnp.zeros((NODES // TS, TS, V), jnp.float32)
    summed, _ = lax.scan(add_device, start, (tile_values.reshape(devices, TILES_DEV, TS, TS), tile_rows.reshape(devices, TILES_DEV), tile_cols.reshape(devices, TILES_DEV), tile_count.reshape(devices), device_ids))
    return summed.reshape(NODES, V) * inv_root[:, None]
```

```python
import jax
import jax.numpy as jnp
from jax import lax
from jax.experimental import pallas as pl
from jax.experimental.pallas import tpu as pltpu
from jax.sharding import PartitionSpec as P

SIDE = 4
FIRST_Y = 344
BUFFERS = 4


def product_kernel(
    rows_ref, cols_ref, count_ref, place_ref, tiles_ref, gathered_ref, *refs
):
    a_outs, b_outs = refs[0:8], refs[8:16]
    acc, tile_buf, vec_buf, tile_sem, vec_sem, out_sem = refs[16:]
    side = tile_buf.shape[1]
    count = count_ref[0]
    my_y = place_ref[0] // SIDE
    my_z = place_ref[0] % SIDE

    def tile_copy(k, slot):
        return pltpu.make_async_copy(tiles_ref.at[k], tile_buf.at[slot], tile_sem.at[slot])

    def vec_copy(k, slot):
        start = pl.multiple_of(cols_ref[k] * side, side)
        return pltpu.make_async_copy(
            gathered_ref.at[pl.ds(start, side)], vec_buf.at[slot], vec_sem.at[slot]
        )

    for k in range(BUFFERS):
        @pl.when(k < count)
        def _():
            tile_copy(k, k).start()
            vec_copy(k, k).start()

    acc[...] = jnp.zeros_like(acc)

    def step(k, carry):
        slot = lax.rem(k, BUFFERS)
        tile_copy(k, slot).wait()
        vec_copy(k, slot).wait()
        vec = vec_buf[slot]
        high = vec.astype(jnp.bfloat16)
        low = (vec - high.astype(jnp.float32)).astype(jnp.bfloat16)
        both = jnp.dot(
            tile_buf[slot],
            jnp.concatenate([high, low], axis=1),
            preferred_element_type=jnp.float32,
        )
        width = vec.shape[1]
        owner = rows_ref[k] // 2
        step_y = lax.rem(owner // SIDE + SIDE - my_y, SIDE)
        step_z = lax.rem(owner % SIDE + SIDE - my_z, SIDE)
        place = (step_y * 2 + rows_ref[k] % 2) * SIDE + step_z
        acc[place] += both[:, :width] + both[:, width:]

        @pl.when(k + BUFFERS < count)
        def _():
            tile_copy(k + BUFFERS, slot).start()
            vec_copy(k + BUFFERS, slot).start()

        return carry

    lax.fori_loop(0, count, step, 0)
    copies = []
    for hop in range(SIDE):
        for half in range(2):
            for other in range(SIDE):
                n = len(copies)
                copies.append(pltpu.make_async_copy(
                    acc.at[(hop * 2 + half) * SIDE + other, pl.ds(0, FIRST_Y)],
                    a_outs[hop * 2 + half].at[other],
                    out_sem.at[n],
                ))
                n = len(copies)
                copies.append(pltpu.make_async_copy(
                    acc.at[(other * 2 + half) * SIDE + hop, pl.ds(FIRST_Y, side - FIRST_Y)],
                    b_outs[hop * 2 + half].at[other],
                    out_sem.at[n],
                ))
    for copy in copies:
        copy.start()
    for copy in copies:
        copy.wait()


def local_product(tile_rows, tile_cols, tile_count, place, tiles, gathered):
    slots, side, _ = tiles.shape
    width = gathered.shape[1]
    a_shape = jax.ShapeDtypeStruct((SIDE, FIRST_Y, width), jnp.float32)
    b_shape = jax.ShapeDtypeStruct((SIDE, side - FIRST_Y, width), jnp.float32)
    smem = pl.BlockSpec(memory_space=pltpu.SMEM)
    hbm = pl.BlockSpec(memory_space=pl.ANY)
    outs = pl.pallas_call(
        product_kernel,
        out_shape=[a_shape] * 8 + [b_shape] * 8,
        in_specs=[smem] * 4 + [hbm] * 2,
        out_specs=[hbm] * 16,
        scratch_shapes=[
            pltpu.VMEM((2 * SIDE * SIDE, side, width), jnp.float32),
            pltpu.VMEM((BUFFERS, side, side), jnp.bfloat16),
            pltpu.VMEM((BUFFERS, side, width), jnp.float32),
            pltpu.SemaphoreType.DMA((BUFFERS,)),
            pltpu.SemaphoreType.DMA((BUFFERS,)),
            pltpu.SemaphoreType.DMA((4 * SIDE * SIDE,)),
        ],
        compiler_params=pltpu.CompilerParams(vmem_limit_bytes=32 * 1024 * 1024),
        cost_estimate=pl.CostEstimate(
            flops=4 * slots * side * side * width,
            bytes_accessed=2 * slots * side * side + 4 * slots * side * width,
            transcendentals=0,
        ),
    )(tile_rows, tile_cols, tile_count, place, tiles, gathered)
    return outs[:8], outs[8:]


def y_shift(step):
    return [
        (y * SIDE + z, ((y + step) % SIDE) * SIDE + z) for y in range(SIDE) for z in range(SIDE)
    ]


def z_shift(step):
    return [(y * SIDE + z, y * SIDE + (z + step) % SIDE) for y in range(SIDE) for z in range(SIDE)]


def ring_sum(parts, shift):
    up = lambda array: lax.ppermute(array, "col", shift(1))
    down = lambda array: lax.ppermute(array, "col", shift(-1))
    far_up, far_down = up(parts[4]), down(parts[5])
    near_up, near_down = up(parts[3]), down(parts[6])
    last_up, last_down = up(parts[2] + far_up), down(parts[7] + far_down)
    return parts[0] + near_down + last_up, parts[1] + near_up + last_down


def split(halves):
    return [halves[half][hop] for hop in range(SIDE) for half in range(2)]


def body(vectors, tile_values, tile_rows, tile_cols, tile_count, degrees):
    row_count = lax.axis_size("row")
    col_count = lax.axis_size("col")
    row_index = lax.axis_index("row")
    col_index = lax.axis_index("col")
    piece_rows = vectors.shape[0]

    def scale(piece):
        own = lax.dynamic_slice_in_dim(degrees, piece * piece_rows, piece_rows)
        return lax.rsqrt(own.astype(jnp.float32))[:, None]

    own_piece = vectors * scale(col_index * row_count + row_index)
    gathered = lax.all_gather(own_piece, "row", axis=0, tiled=True)
    a_parts, b_parts = local_product(
        tile_rows[0, 0], tile_cols[0, 0], tile_count[0], col_index[None], tile_values[0, 0], gathered
    )
    a_y = ring_sum(a_parts, y_shift)
    b_z = ring_sum(b_parts, z_shift)
    a_sum = ring_sum(split(a_y), z_shift)
    b_sum = ring_sum(split(b_z), y_shift)
    result = jnp.concatenate([a_sum[0], b_sum[0], a_sum[1], b_sum[1]], axis=0)
    return result * scale(row_index * col_count + col_index)


def solution(mesh):
    placed = (
        P(("col", "row"), None),
        P("row", "col", None, None, None),
        P("row", "col", None),
        P("row", "col", None),
        P("row", "col"),
        P(),
    )
    return jax.shard_map(
        body, mesh=mesh, in_specs=placed, out_specs=P(("row", "col"), None), check_vma=False
    )
```

```python
import jax
import jax.numpy as jnp
from jax import lax
from jax.experimental import pallas as pl
from jax.experimental.pallas import tpu as pltpu
from jax.sharding import PartitionSpec as P

SIDE = 4
FIRST_Y = 328
BUFFERS = 4
VMEM_LIMIT = 58 * 1024 * 1024


def product_kernel(
    rows_ref, cols_ref, count_ref, place_ref, tiles_ref, gathered_ref, *refs
):
    a_out, b_outs = refs[0], refs[1:9]
    acc, tile_buf, vec_buf, tile_sem, vec_sem, out_sem = refs[9:]
    side = tile_buf.shape[1]
    count = count_ref[0]
    my_y = place_ref[0] // SIDE
    my_z = place_ref[0] % SIDE

    def tile_copy(k, slot):
        return pltpu.make_async_copy(tiles_ref.at[k], tile_buf.at[slot], tile_sem.at[slot])

    def vec_copy(k, slot):
        start = pl.multiple_of(cols_ref[k] * side, side)
        return pltpu.make_async_copy(
            gathered_ref.at[pl.ds(start, side)], vec_buf.at[slot], vec_sem.at[slot]
        )

    for k in range(BUFFERS):
        @pl.when(k < count)
        def _():
            tile_copy(k, k).start()
            vec_copy(k, k).start()

    acc[...] = jnp.zeros_like(acc)

    def step(k, carry):
        slot = lax.rem(k, BUFFERS)
        tile_copy(k, slot).wait()
        vec_copy(k, slot).wait()
        vec = vec_buf[slot]
        high = vec.astype(jnp.bfloat16)
        low = (vec - high.astype(jnp.float32)).astype(jnp.bfloat16)
        both = jnp.dot(
            tile_buf[slot],
            jnp.concatenate([high, low], axis=1),
            preferred_element_type=jnp.float32,
        )
        width = vec.shape[1]
        owner = rows_ref[k] // 2
        step_y = lax.rem(owner // SIDE + SIDE - my_y, SIDE)
        step_z = lax.rem(owner % SIDE + SIDE - my_z, SIDE)
        acc[step_y, step_z, rows_ref[k] % 2] += both[:, :width] + both[:, width:]

        @pl.when(k + BUFFERS < count)
        def _():
            tile_copy(k + BUFFERS, slot).start()
            vec_copy(k + BUFFERS, slot).start()

        return carry

    lax.fori_loop(0, count, step, 0)
    copies = []
    for hop in range(SIDE):
        for half in range(2):
            copies.append(pltpu.make_async_copy(
                acc.at[:, hop, half, pl.ds(FIRST_Y, side - FIRST_Y)],
                b_outs[hop * 2 + half],
                out_sem.at[len(copies)],
            ))
    for hop in range(SIDE):
        copies.append(pltpu.make_async_copy(
            acc.at[hop, :, :, pl.ds(0, FIRST_Y)],
            a_out.at[lax.rem(my_y + hop, SIDE)],
            out_sem.at[len(copies)],
        ))
    for copy in copies:
        copy.start()
    for copy in copies:
        copy.wait()


def local_product(tile_rows, tile_cols, tile_count, place, tiles, gathered):
    slots, side, _ = tiles.shape
    width = gathered.shape[1]
    a_shape = jax.ShapeDtypeStruct((SIDE, SIDE, 2, FIRST_Y, width), jnp.float32)
    b_shape = jax.ShapeDtypeStruct((SIDE, side - FIRST_Y, width), jnp.float32)
    smem = pl.BlockSpec(memory_space=pltpu.SMEM)
    hbm = pl.BlockSpec(memory_space=pl.ANY)
    outs = pl.pallas_call(
        product_kernel,
        out_shape=[a_shape] + [b_shape] * 8,
        in_specs=[smem] * 4 + [hbm] * 2,
        out_specs=[hbm] * 9,
        scratch_shapes=[
            pltpu.VMEM((SIDE, SIDE, 2, side, width), jnp.float32),
            pltpu.VMEM((BUFFERS, side, side), jnp.bfloat16),
            pltpu.VMEM((BUFFERS, side, width), jnp.float32),
            pltpu.SemaphoreType.DMA((BUFFERS,)),
            pltpu.SemaphoreType.DMA((BUFFERS,)),
            pltpu.SemaphoreType.DMA((3 * SIDE,)),
        ],
        compiler_params=pltpu.CompilerParams(vmem_limit_bytes=VMEM_LIMIT),
        cost_estimate=pl.CostEstimate(
            flops=4 * slots * side * side * width,
            bytes_accessed=2 * slots * side * side + 4 * slots * side * width,
            transcendentals=0,
        ),
    )(tile_rows, tile_cols, tile_count, place, tiles, gathered)
    return outs[0], outs[1:]


def y_shift(step):
    return [
        (y * SIDE + z, ((y + step) % SIDE) * SIDE + z) for y in range(SIDE) for z in range(SIDE)
    ]


def z_shift(step):
    return [(y * SIDE + z, y * SIDE + (z + step) % SIDE) for y in range(SIDE) for z in range(SIDE)]


def ring_sum(parts, shift):
    up = lambda array: lax.ppermute(array, "col", shift(1))
    down = lambda array: lax.ppermute(array, "col", shift(-1))
    far_up, far_down = up(parts[4]), down(parts[5])
    near_up, near_down = up(parts[3]), down(parts[6])
    last_up, last_down = up(parts[2] + far_up), down(parts[7] + far_down)
    return parts[0] + near_down + last_up, parts[1] + near_up + last_down


def direct_sum(parts, shift):
    moved = [lax.ppermute(parts[hop], "col", shift(hop)) for hop in range(1, SIDE)]
    return parts[0] + moved[0] + moved[1] + moved[2]


def body(vectors, tile_values, tile_rows, tile_cols, tile_count, degrees):
    row_count = lax.axis_size("row")
    col_count = lax.axis_size("col")
    row_index = lax.axis_index("row")
    col_index = lax.axis_index("col")
    piece_rows = vectors.shape[0]

    def scale(piece):
        own = lax.dynamic_slice_in_dim(degrees, piece * piece_rows, piece_rows)
        return lax.rsqrt(own.astype(jnp.float32))[:, None]

    own_piece = vectors * scale(col_index * row_count + row_index)
    gathered = lax.all_gather(own_piece, "row", axis=0, tiled=True)
    a_parts, b_parts = local_product(
        tile_rows[0, 0], tile_cols[0, 0], tile_count[0], col_index[None], tile_values[0, 0], gathered
    )
    y_groups = [[y * SIDE + z for y in range(SIDE)] for z in range(SIDE)]
    a_y = lax.psum_scatter(
        a_parts, "col", scatter_dimension=0, axis_index_groups=y_groups, tiled=True
    )
    b_z = jnp.stack(ring_sum(b_parts, z_shift), axis=1)
    b_sum = direct_sum(b_z, y_shift)
    a_sum = direct_sum(a_y[0], z_shift)
    result = jnp.concatenate([a_sum, b_sum], axis=1).reshape(piece_rows, vectors.shape[1])
    return result * scale(row_index * col_count + col_index)


def solution(mesh):
    placed = (
        P(("col", "row"), None),
        P("row", "col", None, None, None),
        P("row", "col", None),
        P("row", "col", None),
        P("row", "col"),
        P(),
    )
    return jax.shard_map(
        body, mesh=mesh, in_specs=placed, out_specs=P(("row", "col"), None), check_vma=False
    )
```

```python
import jax
import jax.numpy as jnp
import numpy as np
from jax import lax
from jax.experimental import pallas as pl
from jax.experimental.pallas import tpu as pltpu
from jax.sharding import PartitionSpec as P

SIDE = 4
FIRST_Y = 344
BUFFERS = 4
VMEM_LIMIT = 58 * 1024 * 1024
SOURCES = 16
SOURCE_REF = np.array([0, 0, 1, 1, 3, 3, 5, 5, 4, 5, 6, 7, 2, 2, 4, 4], np.int32)
SOURCE_TILE = np.array([0, 1, 0, 1, 0, 1, 0, 1, 2, 2, 0, 0, 0, 1, 0, 1], np.int32)


def product_kernel(ref_ids, tile_ids, places, count_ref, tiles_ref, *refs):
    sources, outs = refs[:SOURCES], refs[SOURCES:-6]
    acc, tile_buf, vec_buf, tile_sem, vec_sem, out_sem = refs[-6:]
    side = tile_buf.shape[1]
    count = count_ref[0]

    def tile_copy(k, slot):
        return pltpu.make_async_copy(tiles_ref.at[k], tile_buf.at[slot], tile_sem.at[slot])

    def vec_copy(ref, start, slot):
        return pltpu.make_async_copy(
            ref.at[pl.ds(start, side)], vec_buf.at[slot], vec_sem.at[slot]
        )

    def start(k, slot):
        tile_copy(k, slot).start()
        first = pl.multiple_of(tile_ids[k] * side, side)
        for n, source in enumerate(sources):
            @pl.when(ref_ids[k] == n)
            def _(source=source):
                vec_copy(source, first, slot).start()

    for k in range(BUFFERS):
        @pl.when(k < count)
        def _(k=k):
            start(k, k)

    acc[...] = jnp.zeros_like(acc)

    def step(k, carry):
        slot = lax.rem(k, BUFFERS)
        tile_copy(k, slot).wait()
        vec_copy(sources[0], 0, slot).wait()
        vec = vec_buf[slot]
        high = vec.astype(jnp.bfloat16)
        low = (vec - high.astype(jnp.float32)).astype(jnp.bfloat16)
        both = jnp.dot(
            tile_buf[slot],
            jnp.concatenate([high, low], axis=1),
            preferred_element_type=jnp.float32,
        )
        width = vec.shape[1]
        step_y, step_z, half = places[k] // 8, places[k] // 2 % SIDE, places[k] % 2
        acc[step_y, step_z, half] += both[:, :width] + both[:, width:]

        @pl.when(k + BUFFERS < count)
        def _():
            start(k + BUFFERS, slot)

        return carry

    lax.fori_loop(0, count, step, 0)

    def pieces(at, up, down, late_up, late_down, own):
        return [
            (at(2, 0), up.at[0]),
            (at(1, 1), up.at[1]),
            (at(2, 1), down.at[0]),
            (at(3, 0), down.at[1]),
            (at(1, 0), late_up),
            (at(3, 1), late_down),
            (at(0, 0), own.at[0]),
            (at(0, 1), own.at[1]),
        ]

    top, bottom = pl.ds(0, FIRST_Y), pl.ds(FIRST_Y, side - FIRST_Y)
    pairs = pieces(lambda hop, half: acc.at[hop, :, half, top], *outs[:5])
    pairs += pieces(lambda hop, half: acc.at[:, hop, half, bottom], *outs[5:])
    copies = [
        pltpu.make_async_copy(source, target, out_sem.at[n])
        for n, (source, target) in enumerate(pairs)
    ]
    for copy in copies:
        copy.start()
    for copy in copies:
        copy.wait()


def local_product(ref_ids, tile_ids, places, tile_count, tiles, sources):
    slots, side, _ = tiles.shape
    width = sources[0].shape[1]
    smem = pl.BlockSpec(memory_space=pltpu.SMEM)
    hbm = pl.BlockSpec(memory_space=pl.ANY)
    shapes = []
    for rows in (FIRST_Y, side - FIRST_Y):
        half = (SIDE, rows, width)
        shapes += [(2, *half), (2, *half), half, half, (2, *half)]
    outs = pl.pallas_call(
        product_kernel,
        out_shape=[jax.ShapeDtypeStruct(shape, jnp.float32) for shape in shapes],
        in_specs=[smem] * 4 + [hbm] * (1 + SOURCES),
        out_specs=[hbm] * 10,
        scratch_shapes=[
            pltpu.VMEM((SIDE, SIDE, 2, side, width), jnp.float32),
            pltpu.VMEM((BUFFERS, side, side), jnp.bfloat16),
            pltpu.VMEM((BUFFERS, side, width), jnp.float32),
            pltpu.SemaphoreType.DMA((BUFFERS,)),
            pltpu.SemaphoreType.DMA((BUFFERS,)),
            pltpu.SemaphoreType.DMA((4 * SIDE,)),
        ],
        compiler_params=pltpu.CompilerParams(vmem_limit_bytes=VMEM_LIMIT),
        cost_estimate=pl.CostEstimate(
            flops=4 * slots * side * side * width,
            bytes_accessed=2 * slots * side * side + 4 * slots * side * width,
            transcendentals=0,
        ),
    )(ref_ids, tile_ids, places, tile_count, tiles, *sources)
    return outs[:5], outs[5:]


def y_shift(step):
    return [
        (y * SIDE + z, ((y + step) % SIDE) * SIDE + z) for y in range(SIDE) for z in range(SIDE)
    ]


def z_shift(step):
    return [(y * SIDE + z, y * SIDE + (z + step) % SIDE) for y in range(SIDE) for z in range(SIDE)]


def x_shift(step):
    return y_shift(step)


def flip(bit):
    return [(i, i ^ bit) for i in range(SIDE * SIDE)]


def row_gather(piece, side):
    right = lambda array: lax.ppermute(array, "row", x_shift(1))
    left = lambda array: lax.ppermute(array, "row", x_shift(-1))
    other = lax.ppermute(piece, "row", flip(2))
    from_left, from_right = right(piece), left(piece)
    far_left = right(jnp.concatenate([other, from_left[:side]]))
    far_right = left(jnp.concatenate([other, from_right[side:]]))
    last_left, last_right = right(far_left[:side]), left(far_right[side : 2 * side])
    mine = [piece, other, from_left, from_right, far_left, far_right, last_left, last_right]
    return mine + [lax.ppermute(array, "row", flip(1)) for array in mine]


def ring_sum(up, down, late_up, late_down, own, shift):
    from_below = lax.ppermute(up, "col", shift(1))
    from_above = lax.ppermute(down, "col", shift(-1))
    last_below = lax.ppermute(late_up + from_below[0], "col", shift(1))
    last_above = lax.ppermute(late_down + from_above[0], "col", shift(-1))
    return own[0] + from_above[1] + last_below, own[1] + from_below[1] + last_above


def direct_sum(parts, shift):
    moved = [lax.ppermute(parts[hop], "col", shift(hop)) for hop in range(1, SIDE)]
    return parts[0] + moved[0] + moved[1] + moved[2]


def body(vectors, tile_values, tile_rows, tile_cols, tile_count, degrees):
    row_count = lax.axis_size("row")
    col_count = lax.axis_size("col")
    row = lax.axis_index("row")
    col = lax.axis_index("col")
    piece_rows, width = vectors.shape
    side = tile_values.shape[-1]

    def scale(piece):
        own = lax.dynamic_slice_in_dim(degrees, piece * piece_rows, piece_rows)
        return lax.rsqrt(own.astype(jnp.float32))[:, None]

    sources = row_gather(vectors * scale(col * row_count + row), side)

    owner = tile_cols[0, 0] // 2
    step_x = (owner // SIDE - row // SIDE) % SIDE
    other_z = (owner // 2 + row // 2) % 2
    index = (step_x * 2 + other_z) * 2 + tile_cols[0, 0] % 2
    ref_ids = jnp.asarray(SOURCE_REF)[index] + SOURCES // 2 * ((owner + row) % 2)
    tile_ids = jnp.asarray(SOURCE_TILE)[index]
    target = tile_rows[0, 0] // 2
    step_y = (target // SIDE - col // SIDE) % SIDE
    step_z = (target - col) % SIDE
    places = (step_y * SIDE + step_z) * 2 + tile_rows[0, 0] % 2

    a_parts, b_parts = local_product(
        ref_ids, tile_ids, places, tile_count[0], tile_values[0, 0], sources
    )
    a_y = jnp.stack(ring_sum(*a_parts, y_shift), axis=1)
    b_z = jnp.stack(ring_sum(*b_parts, z_shift), axis=1)
    b_sum = direct_sum(b_z, y_shift)
    a_sum = direct_sum(a_y, z_shift)
    result = jnp.concatenate([a_sum, b_sum], axis=1).reshape(piece_rows, width)
    return result * scale(row * col_count + col)


def solution(mesh):
    placed = (
        P(("col", "row"), None),
        P("row", "col", None, None, None),
        P("row", "col", None),
        P("row", "col", None),
        P("row", "col"),
        P(),
    )
    return jax.shard_map(
        body, mesh=mesh, in_specs=placed, out_specs=P(("row", "col"), None), check_vma=False
    )
```

```python
import jax
import jax.numpy as jnp
from jax import lax
from jax.experimental import pallas as pl
from jax.experimental.pallas import tpu as pltpu
from jax.sharding import PartitionSpec as P

SIDE = 4
SEGMENTS = (("y", 328), ("z", 184))
BUFFERS = 4
VMEM_LIMIT = 40 * 1024 * 1024
SOURCES = 20
SOURCE_REF = (0, 0, 1, 1, 3, 3, 7, 6, 5, 7, 8, 9, 2, 2, 4, 5)
SOURCE_TILE = (0, 1, 0, 1, 0, 1, 0, 0, 1, 1, 0, 0, 0, 1, 0, 0)


def table(values, index):
    low, high = (sum(v << 4 * i for i, v in enumerate(values[n : n + 8])) for n in (0, 8))
    word = jnp.where(index < 8, jnp.int32(signed(low)), jnp.int32(signed(high)))
    return lax.shift_right_logical(word, 4 * (index % 8)) & 15


def signed(word):
    return word - (1 << 32) if word >> 31 else word


def product_kernel(rows_ref, cols_ref, count_ref, tiles_ref, *refs):
    sources, outs = refs[:SOURCES], refs[SOURCES:-6]
    acc, tile_buf, vec_buf, tile_sem, vec_sem, out_sem = refs[-6:]
    side = tile_buf.shape[1]
    count = count_ref[0]
    row, col = lax.axis_index("row"), lax.axis_index("col")

    def tile_copy(k, slot):
        return pltpu.make_async_copy(tiles_ref.at[k], tile_buf.at[slot], tile_sem.at[slot])

    def vec_copy(ref, start, slot):
        return pltpu.make_async_copy(
            ref.at[pl.ds(start, side)], vec_buf.at[slot], vec_sem.at[slot]
        )

    def start(k, slot):
        tile_copy(k, slot).start()
        owner = cols_ref[k] // 2
        step_x = (owner // SIDE + SIDE - row // SIDE) % SIDE
        other_z = (owner // 2 + row // 2) % 2
        index = (step_x * 2 + other_z) * 2 + cols_ref[k] % 2
        ref_id = table(SOURCE_REF, index) + SOURCES // 2 * ((owner + row) % 2)
        first = pl.multiple_of(table(SOURCE_TILE, index) * side, side)
        for n, source in enumerate(sources):
            @pl.when(ref_id == n)
            def _(source=source):
                vec_copy(source, first, slot).start()

    for k in range(BUFFERS):
        @pl.when(k < count)
        def _(k=k):
            start(k, k)

    acc[...] = jnp.zeros_like(acc)

    def step(k, carry):
        slot = lax.rem(k, BUFFERS)
        tile_copy(k, slot).wait()
        vec_copy(sources[0], 0, slot).wait()
        vec = vec_buf[slot]
        high = vec.astype(jnp.bfloat16)
        low = (vec - high.astype(jnp.float32)).astype(jnp.bfloat16)
        both = jnp.dot(
            tile_buf[slot],
            jnp.concatenate([high, low], axis=1),
            preferred_element_type=jnp.float32,
        )
        width = vec.shape[1]
        owner = rows_ref[k] // 2
        step_y = (owner // SIDE + SIDE - col // SIDE) % SIDE
        step_z = (owner + SIDE - col % SIDE) % SIDE
        acc[step_y, step_z, rows_ref[k] % 2] += both[:, :width] + both[:, width:]

        @pl.when(k + BUFFERS < count)
        def _():
            start(k + BUFFERS, slot)

        return carry

    lax.fori_loop(0, count, step, 0)

    def pieces(at, up, down, late_up, late_down, own):
        return [
            (at(2, 0), up.at[0]),
            (at(1, 1), up.at[1]),
            (at(2, 1), down.at[0]),
            (at(3, 0), down.at[1]),
            (at(1, 0), late_up),
            (at(3, 1), late_down),
            (at(0, 0), own.at[0]),
            (at(0, 1), own.at[1]),
        ]

    pairs, first = [], 0
    for n, (way, rows) in enumerate(SEGMENTS):
        part = pl.ds(first, rows)
        if way == "y":
            at = lambda hop, half, part=part: acc.at[hop, :, half, part]
        else:
            at = lambda hop, half, part=part: acc.at[:, hop, half, part]
        pairs += pieces(at, *outs[5 * n : 5 * n + 5])
        first += rows
    copies = [
        pltpu.make_async_copy(source, target, out_sem.at[n])
        for n, (source, target) in enumerate(pairs)
    ]
    for copy in copies:
        copy.start()
    for copy in copies:
        copy.wait()


def local_product(tile_rows, tile_cols, tile_count, tiles, sources):
    slots, side, _ = tiles.shape
    width = sources[0].shape[1]
    smem = pl.BlockSpec(memory_space=pltpu.SMEM)
    hbm = pl.BlockSpec(memory_space=pl.ANY)
    shapes = []
    for _, rows in SEGMENTS:
        half = (SIDE, rows, width)
        shapes += [(2, *half), (2, *half), half, half, (2, *half)]
    outs = pl.pallas_call(
        product_kernel,
        out_shape=[jax.ShapeDtypeStruct(shape, jnp.float32) for shape in shapes],
        in_specs=[smem] * 3 + [hbm] + [hbm] * SOURCES,
        out_specs=[hbm] * len(shapes),
        scratch_shapes=[
            pltpu.VMEM((SIDE, SIDE, 2, side, width), jnp.float32),
            pltpu.VMEM((BUFFERS, side, side), jnp.bfloat16),
            pltpu.VMEM((BUFFERS, side, width), jnp.float32),
            pltpu.SemaphoreType.DMA((BUFFERS,)),
            pltpu.SemaphoreType.DMA((BUFFERS,)),
            pltpu.SemaphoreType.DMA((8 * len(SEGMENTS),)),
        ],
        compiler_params=pltpu.CompilerParams(vmem_limit_bytes=VMEM_LIMIT),
        cost_estimate=pl.CostEstimate(
            flops=4 * slots * side * side * width,
            bytes_accessed=2 * slots * side * side + 4 * slots * side * width,
            transcendentals=0,
        ),
    )(tile_rows, tile_cols, tile_count, tiles, *sources)
    return [outs[5 * n : 5 * n + 5] for n in range(len(SEGMENTS))]


def y_shift(step):
    return [
        (y * SIDE + z, ((y + step) % SIDE) * SIDE + z) for y in range(SIDE) for z in range(SIDE)
    ]


def z_shift(step):
    return [(y * SIDE + z, y * SIDE + (z + step) % SIDE) for y in range(SIDE) for z in range(SIDE)]


def x_shift(step):
    return y_shift(step)


def flip(bit):
    return [(i, i ^ bit) for i in range(SIDE * SIDE)]


def row_gather(piece, side):
    right = lambda array: lax.ppermute(array, "row", x_shift(1))
    left = lambda array: lax.ppermute(array, "row", x_shift(-1))
    other = lax.ppermute(piece, "row", flip(2))
    from_left, from_right = right(piece), left(piece)
    near_left, near_right = right(other[:side]), left(other[side:])
    far_left = right(jnp.concatenate([other[side:], from_left[:side]]))
    far_right = left(jnp.concatenate([other[:side], from_right[side:]]))
    core = lambda array: lax.ppermute(array, "row", flip(1))
    first = [piece, other, from_left, from_right]
    near_left, near_right, first = lax.optimization_barrier((near_left, near_right, first))
    last = [right(near_left), left(near_right)]
    others = [core(array) for array in first]
    near_left, far_left, near_right, far_right = lax.optimization_barrier(
        (near_left, far_left, near_right, far_right)
    )
    second = [near_left, far_left, near_right, far_right]
    return first + second + last + others + [core(array) for array in second + last]


def ring_sum(up, down, late_up, late_down, own, shift):
    from_below = lax.ppermute(up, "col", shift(1))
    from_above = lax.ppermute(down, "col", shift(-1))
    last_below = lax.ppermute(late_up + from_below[0], "col", shift(1))
    last_above = lax.ppermute(late_down + from_above[0], "col", shift(-1))
    return own[0] + from_above[1] + last_below, own[1] + from_below[1] + last_above


def direct_sum(parts, shift):
    moved = [lax.ppermute(parts[hop], "col", shift(hop)) for hop in range(1, SIDE)]
    return parts[0] + moved[0] + moved[1] + moved[2]


def pair_sum(parts):
    pairs = lambda step: [
        (y * SIDE + z, (y + (step if y % 2 == 0 else -step)) % SIDE * SIDE + z)
        for y in range(SIDE)
        for z in range(SIDE)
    ]
    even = lax.axis_index("col") // SIDE % 2 == 0
    near, far = jnp.where(even, parts[1], parts[3]), jnp.where(even, parts[3], parts[1])
    got = lax.ppermute(jnp.stack([near, parts[2]]), "col", pairs(1))
    return parts[0] + got[0] + lax.ppermute(far + got[1], "col", pairs(-1))


def body(vectors, tile_values, tile_rows, tile_cols, tile_count, degrees):
    row_count = lax.axis_size("row")
    col_count = lax.axis_size("col")
    row = lax.axis_index("row")
    col = lax.axis_index("col")
    piece_rows, width = vectors.shape
    side = tile_values.shape[-1]

    def scale(piece):
        own = lax.dynamic_slice_in_dim(degrees, piece * piece_rows, piece_rows)
        return lax.rsqrt(own.astype(jnp.float32))[:, None]

    sources = row_gather(vectors * scale(col * row_count + row), side)

    segments = local_product(
        tile_rows[0, 0], tile_cols[0, 0], tile_count[0], tile_values[0, 0], sources
    )
    shifts = {"y": y_shift, "z": z_shift}
    middle = [
        jnp.stack(ring_sum(*parts, shifts[way]), axis=1)
        for parts, (way, _) in zip(segments, SEGMENTS)
    ]
    middle = lax.optimization_barrier(middle)
    sums = [direct_sum(middle[0], z_shift), pair_sum(middle[1])]
    result = jnp.concatenate(sums, axis=1).reshape(piece_rows, width)
    return result * scale(row * col_count + col)


def solution(mesh):
    placed = (
        P(("col", "row"), None),
        P("row", "col", None, None, None),
        P("row", "col", None),
        P("row", "col", None),
        P("row", "col"),
        P(),
    )
    return jax.shard_map(
        body, mesh=mesh, in_specs=placed, out_specs=P(("row", "col"), None), check_vma=False
    )
```

```python
import jax
import jax.numpy as jnp
from jax import lax
from jax.experimental import pallas as pl
from jax.experimental.pallas import tpu as pltpu
from jax.sharding import PartitionSpec as P

SIDE = 4
SEGMENTS = (("y", 352), ("z", 160))
BUFFERS = 4
VMEM_LIMIT = 58 * 1024 * 1024
SOURCES = 20
SOURCE_REF = (0, 0, 1, 1, 3, 3, 7, 6, 5, 7, 8, 9, 2, 2, 4, 5)
SOURCE_TILE = (0, 1, 0, 1, 0, 1, 0, 0, 1, 1, 0, 0, 0, 1, 0, 0)


def table(values, index):
    low, high = (sum(v << 4 * i for i, v in enumerate(values[n : n + 8])) for n in (0, 8))
    word = jnp.where(index < 8, jnp.int32(signed(low)), jnp.int32(signed(high)))
    return lax.shift_right_logical(word, 4 * (index % 8)) & 15


def signed(word):
    return word - (1 << 32) if word >> 31 else word


def product_kernel(rows_ref, cols_ref, count_ref, tiles_ref, *refs):
    sources, outs = refs[:SOURCES], refs[SOURCES:-6]
    acc, tile_buf, vec_buf, tile_sem, vec_sem, out_sem = refs[-6:]
    side = tile_buf.shape[1]
    count = count_ref[0]
    row, col = lax.axis_index("row"), lax.axis_index("col")

    def tile_copy(k, slot):
        return pltpu.make_async_copy(tiles_ref.at[k], tile_buf.at[slot], tile_sem.at[slot])

    def vec_copy(ref, start, slot):
        return pltpu.make_async_copy(
            ref.at[pl.ds(start, side)], vec_buf.at[slot], vec_sem.at[slot]
        )

    def start(k, slot):
        tile_copy(k, slot).start()
        owner = cols_ref[k] // 2
        step_x = (owner // SIDE + SIDE - row // SIDE) % SIDE
        other_z = (owner // 2 + row // 2) % 2
        index = (step_x * 2 + other_z) * 2 + cols_ref[k] % 2
        ref_id = table(SOURCE_REF, index) + SOURCES // 2 * ((owner + row) % 2)
        first = pl.multiple_of(table(SOURCE_TILE, index) * side, side)
        for n, source in enumerate(sources):
            @pl.when(ref_id == n)
            def _(source=source):
                vec_copy(source, first, slot).start()

    for k in range(BUFFERS):
        @pl.when(k < count)
        def _(k=k):
            start(k, k)

    acc[...] = jnp.zeros_like(acc)

    def step(k, carry):
        slot = lax.rem(k, BUFFERS)
        tile_copy(k, slot).wait()
        vec_copy(sources[0], 0, slot).wait()
        vec = vec_buf[slot]
        high = vec.astype(jnp.bfloat16)
        low = (vec - high.astype(jnp.float32)).astype(jnp.bfloat16)
        both = jnp.dot(
            tile_buf[slot],
            jnp.concatenate([high, low], axis=1),
            preferred_element_type=jnp.float32,
        )
        width = vec.shape[1]
        owner = rows_ref[k] // 2
        step_y = (owner // SIDE + SIDE - col // SIDE) % SIDE
        step_z = (owner + SIDE - col % SIDE) % SIDE
        acc[step_y, step_z, rows_ref[k] % 2] += both[:, :width] + both[:, width:]

        @pl.when(k + BUFFERS < count)
        def _():
            start(k + BUFFERS, slot)

        return carry

    lax.fori_loop(0, count, step, 0)

    def pieces(at, up, down, late_up, late_down, own):
        return [
            (at(2, 0), up.at[0]),
            (at(1, 1), up.at[1]),
            (at(2, 1), down.at[0]),
            (at(3, 0), down.at[1]),
            (at(1, 0), late_up),
            (at(3, 1), late_down),
            (at(0, 0), own.at[0]),
            (at(0, 1), own.at[1]),
        ]

    pairs, first = [], 0
    for n, (way, rows) in enumerate(SEGMENTS):
        part = pl.ds(first, rows)
        if way == "y":
            at = lambda hop, half, part=part: acc.at[hop, :, half, part]
        else:
            at = lambda hop, half, part=part: acc.at[:, hop, half, part]
        pairs += pieces(at, *outs[5 * n : 5 * n + 5])
        first += rows
    copies = [
        pltpu.make_async_copy(source, target, out_sem.at[n])
        for n, (source, target) in enumerate(pairs)
    ]
    for copy in copies:
        copy.start()
    for copy in copies:
        copy.wait()


def local_product(tile_rows, tile_cols, tile_count, tiles, sources):
    slots, side, _ = tiles.shape
    width = sources[0].shape[1]
    smem = pl.BlockSpec(memory_space=pltpu.SMEM)
    hbm = pl.BlockSpec(memory_space=pl.ANY)
    shapes = []
    for _, rows in SEGMENTS:
        half = (SIDE, rows, width)
        shapes += [(2, *half), (2, *half), half, half, (2, *half)]
    outs = pl.pallas_call(
        product_kernel,
        out_shape=[jax.ShapeDtypeStruct(shape, jnp.float32) for shape in shapes],
        in_specs=[smem] * 3 + [hbm] * (1 + SOURCES),
        out_specs=[hbm] * len(shapes),
        scratch_shapes=[
            pltpu.VMEM((SIDE, SIDE, 2, side, width), jnp.float32),
            pltpu.VMEM((BUFFERS, side, side), jnp.bfloat16),
            pltpu.VMEM((BUFFERS, side, width), jnp.float32),
            pltpu.SemaphoreType.DMA((BUFFERS,)),
            pltpu.SemaphoreType.DMA((BUFFERS,)),
            pltpu.SemaphoreType.DMA((8 * len(SEGMENTS),)),
        ],
        compiler_params=pltpu.CompilerParams(vmem_limit_bytes=VMEM_LIMIT),
        cost_estimate=pl.CostEstimate(
            flops=4 * slots * side * side * width,
            bytes_accessed=2 * slots * side * side + 4 * slots * side * width,
            transcendentals=0,
        ),
    )(tile_rows, tile_cols, tile_count, tiles, *sources)
    return [outs[5 * n : 5 * n + 5] for n in range(len(SEGMENTS))]


def y_shift(step):
    return [
        (y * SIDE + z, ((y + step) % SIDE) * SIDE + z) for y in range(SIDE) for z in range(SIDE)
    ]


def z_shift(step):
    return [(y * SIDE + z, y * SIDE + (z + step) % SIDE) for y in range(SIDE) for z in range(SIDE)]


def x_shift(step):
    return y_shift(step)


def flip(bit):
    return [(i, i ^ bit) for i in range(SIDE * SIDE)]


def row_gather(piece, side):
    right = lambda array: lax.ppermute(array, "row", x_shift(1))
    left = lambda array: lax.ppermute(array, "row", x_shift(-1))
    other = lax.ppermute(piece, "row", flip(2))
    from_left, from_right = right(piece), left(piece)
    near_left, near_right = right(other[:side]), left(other[side:])
    far_left = right(jnp.concatenate([other[side:], from_left[:side]]))
    far_right = left(jnp.concatenate([other[:side], from_right[side:]]))
    core = lambda array: lax.ppermute(array, "row", flip(1))
    first = [piece, other, from_left, from_right]
    near_left, near_right, first = lax.optimization_barrier((near_left, near_right, first))
    last = [right(near_left), left(near_right)]
    others = [core(array) for array in first]
    near_left, far_left, near_right, far_right = lax.optimization_barrier(
        (near_left, far_left, near_right, far_right)
    )
    second = [near_left, far_left, near_right, far_right]
    return first + second + last + others + [core(array) for array in second + last]


def ring_first(up, down, shift):
    return lax.ppermute(up, "col", shift(1)), lax.ppermute(down, "col", shift(-1))


def ring_late(below, above, late_up, late_down, shift):
    return (
        lax.ppermute(late_up + below[0], "col", shift(1)),
        lax.ppermute(late_down + above[0], "col", shift(-1)),
    )


def ring_total(own, first, late):
    return jnp.stack([own[0] + first[1][1] + late[0], own[1] + first[0][1] + late[1]], axis=1)


def direct_moves(parts, shift):
    return [lax.ppermute(parts[hop], "col", shift(hop)) for hop in range(1, SIDE)]


def pair_sum(parts):
    pairs = lambda step: [
        (y * SIDE + z, (y + (step if y % 2 == 0 else -step)) % SIDE * SIDE + z)
        for y in range(SIDE)
        for z in range(SIDE)
    ]
    even = lax.axis_index("col") // SIDE % 2 == 0
    near, far = jnp.where(even, parts[1], parts[3]), jnp.where(even, parts[3], parts[1])
    got = lax.ppermute(jnp.stack([near, parts[2]]), "col", pairs(1))
    return parts[0] + got[0] + lax.ppermute(far + got[1], "col", pairs(-1))


def body(vectors, tile_values, tile_rows, tile_cols, tile_count, degrees):
    row_count = lax.axis_size("row")
    col_count = lax.axis_size("col")
    row = lax.axis_index("row")
    col = lax.axis_index("col")
    piece_rows, width = vectors.shape
    side = tile_values.shape[-1]

    def scale(piece):
        own = lax.dynamic_slice_in_dim(degrees, piece * piece_rows, piece_rows)
        return lax.rsqrt(own.astype(jnp.float32))[:, None]

    sources = row_gather(vectors * scale(col * row_count + row), side)

    segments = local_product(
        tile_rows[0, 0], tile_cols[0, 0], tile_count[0], tile_values[0, 0], sources
    )
    (a_up, a_down, *a_late, a_own), (b_up, b_down, *b_late, b_own) = segments
    a_first = ring_first(a_up, a_down, y_shift)
    b_first = ring_first(b_up, b_down, z_shift)
    a_tied, b_first = lax.optimization_barrier((a_first, b_first))
    a_last = ring_late(*a_first, *a_late, y_shift)
    b_last = ring_late(*b_first, *b_late, z_shift)
    a_middle = ring_total(a_own, a_tied, a_last)
    moved = direct_moves(a_middle, z_shift)
    b_middle = ring_total(b_own, b_first, b_last)
    own, b_middle = lax.optimization_barrier((a_middle[0], b_middle))
    sums = [own + moved[0] + moved[1] + moved[2], pair_sum(b_middle)]
    result = jnp.concatenate(sums, axis=1).reshape(piece_rows, width)
    return result * scale(row * col_count + col)


def solution(mesh):
    placed = (
        P(("col", "row"), None),
        P("row", "col", None, None, None),
        P("row", "col", None),
        P("row", "col", None),
        P("row", "col"),
        P(),
    )
    return jax.shard_map(
        body, mesh=mesh, in_specs=placed, out_specs=P(("row", "col"), None), check_vma=False
    )
```
